128 devices in a mesh: dp: 16 (over y, z), cent: 8 (over x, core).
Axes of the slice: x: 4, y: 4, z: 4, core: 2. Of those that a mesh axis runs over, the one named last changes fastest.
Arguments:
- points: bfloat16 [65536, 1024], P(('dp', 'cent')), may hold values from -10 to 10
- candidates: int32 [1024, 2], P(('dp', 'cent')), may hold values from 0 to 15, all different within a row; in each aligned block of 8 rows (0 to 7, 8 to 15, ...) at most 2 rows name the same one
- level_one: bfloat16 [32768, 1024], P(('dp', 'cent')), may hold values from -6 to 6
- level_two: bfloat16 [2048, 1024], P(('dp', 'cent')), may hold values from -6 to 6
Outputs:
- level_one_next: float32 [32768, 1024], P(('dp', 'cent'))
- level_two_next: float32 [2048, 1024], P(('dp', 'cent'))
The draws below stay inside these ranges and needn't reach their ends.
Inputs may be any that keep to these rules, and one draw needn't show every extreme that they name: `candidates`: among the 8 rows of one device no group is named more than 2 times, and in every draw some device names some group exactly 2 times; the two groups of a row differ.
All inputs are finite; a program needn't handle non-finite values.
Results may differ from the reference program's by a relative error of at most 0.0004.
Values may be sent and summed in bfloat16 or wider, within the bound.
A program may use at most 128 MiB of HBM per device.

```python
import math
import jax
import jax.numpy as jnp
import numpy as np
from jax import lax

D = 1024
PBS = 64
PB = 8
CAP = 2
NPB = 1024
NP = 65536
CBLK = 2048
K1 = 32768
K2 = 2048
N_DP = 16


def draw_points(key, part):
    noise_key = jax.random.fold_in(key, 11)
    values = jnp.clip(jax.random.normal(noise_key, (NP, D), jnp.float32), -6.0, 6.0)
    return values.astype(jnp.bfloat16)


def draw_level_one(key, part):
    noise_key = jax.random.fold_in(key, 21)
    values = jnp.clip(jax.random.normal(noise_key, (K1, D), jnp.float32), -6.0, 6.0)
    return values.astype(jnp.bfloat16)


def draw_level_two(key, part):
    noise_key = jax.random.fold_in(key, 31)
    values = jnp.clip(jax.random.normal(noise_key, (K2, D), jnp.float32), -6.0, 6.0)
    return values.astype(jnp.bfloat16)


def deal_out(rng, own, number, rows, number_of, top, limit, lean):
    order = jax.random.permutation(rng, number_of)
    crowded, common = portions_of(number_of, rows * top, limit, lean, True), portions_of(number_of, rows * top, limit, lean, False)
    places = jnp.arange(number_of)

    def named(lengths, offset_by):
        used = int((lengths > 0).sum())
        fixed = max(1, used // 4)
        shifted = fixed + (places - fixed + offset_by * (used - fixed)) % max(1, number_of - fixed)
        return jnp.zeros((number_of,), jnp.int32).at[order[jnp.where(places < fixed, places, shifted)]].set(jnp.asarray(lengths, jnp.int32))

    lengths = jnp.where(number % 4 == 0, named(crowded, number // 4), named(common, number - number // 4 - 1))
    mixed = jax.random.permutation(jax.random.fold_in(own, 3), number_of)
    source_of, sink = mixed[0:number_of // 2 * 2:2], mixed[1:number_of // 2 * 2:2]
    slack = jnp.minimum(lengths[source_of] - 1, limit - lengths[sink]) // 2
    slack = jnp.where((source_of == order[0]) | (sink == order[0]) | (lengths[sink] == 0), 0, jnp.maximum(slack, 0))
    shifted = jax.random.randint(jax.random.fold_in(own, 4), (number_of // 2,), 0, 1 << 20) % (slack + 1)
    lengths = lengths.at[source_of].add(-shifted).at[sink].add(shifted)
    items = jnp.searchsorted(jnp.cumsum(lengths), jnp.arange(rows * top), side="right").astype(jnp.int32)
    grid = items.reshape(top, rows).T
    grid = grid[jax.random.permutation(jax.random.fold_in(own, 1), rows)]
    offset_by = jax.random.randint(jax.random.fold_in(own, 2), (rows, 1), 0, top)
    return jnp.take_along_axis(grid, (jnp.arange(top)[None, :] + offset_by) % top, axis=1)


def portions_of(amount, total, most, lean, full):
    portions = [(1 << 20) // math.isqrt(grade ** lean) + 1 for grade in range(1, amount + 1)]
    largest = most if full else min(most, max(-(-total // amount), total * portions[0] // sum(portions)))
    least = 1 if total - largest >= amount - 1 else 0
    holding, surplus = [largest] + [least] * (amount - 1), total - largest - least * (amount - 1)
    while surplus > 0:
        free = [i for i in range(1, amount) if holding[i] < largest] or [i for i in range(1, amount) if holding[i] < most]
        whole, remaining = sum([portions[i] for i in free]), surplus
        for i in free:
            extra = min(most - holding[i], max(1, remaining * portions[i] // whole), surplus)
            holding[i] = holding[i] + extra
            surplus = surplus - extra
    return np.array(holding)


def setup_inputs(seed: int = 0) -> dict:
    seeds = jax.random.split(jax.random.key(seed), 5)
    points = draw_points(jax.random.fold_in(seeds[4], 71), 0)
    candidates_keys = jax.random.split(jax.random.fold_in(seeds[1], 1), NPB // PB)
    candidates_turns = jax.random.permutation(jax.random.fold_in(seeds[1], 3), NPB // PB)
    candidates = jax.vmap(lambda own, number: deal_out(jax.random.fold_in(seeds[1], 2), own, number, PB, N_DP, 2, CAP, 2))(candidates_keys, candidates_turns).reshape((NPB, 2))
    level_one = draw_level_one(jax.random.fold_in(seeds[4], 71), 0)
    level_two = draw_level_two(jax.random.fold_in(seeds[4], 71), 0)
    return dict(points=points, candidates=candidates, level_one=level_one, level_two=level_two)


prior_mass = 1.0


def reference(points, candidates, level_one, level_two):
    temp_one = D / 16.0
    temp_two = D / 64.0
    highest = lax.Precision.HIGHEST
    point_blocks = points.reshape(NPB, PBS, D)

    def one_block(carry, item):
        weighted_sums, mass_total = carry
        point_block, cand_pair = item
        start_a = (cand_pair[0] * CBLK).astype(jnp.int32)
        start_b = (cand_pair[1] * CBLK).astype(jnp.int32)
        rows_a = lax.dynamic_slice_in_dim(level_one, start_a, CBLK, 0)
        rows_b = lax.dynamic_slice_in_dim(level_one, start_b, CBLK, 0)
        candidate_rows = jnp.concatenate([rows_a, rows_b], 0)
        squares = jnp.sum(jnp.square(candidate_rows.astype(jnp.float32)), 1)
        products = lax.dot_general(point_block, candidate_rows, (((1,), (1,)), ((), ())), preferred_element_type=jnp.float32)
        scores = (2.0 * products - squares[None, :]) / temp_one
        log_total = jax.nn.logsumexp(scores, axis=1, keepdims=True)
        weights = jnp.exp(scores - log_total).astype(jnp.bfloat16)
        block_sums = lax.dot_general(weights, point_block, (((0,), (0,)), ((), ())), preferred_element_type=jnp.float32)
        block_mass = jnp.sum(weights.astype(jnp.float32), 0)
        for which, start in ((0, start_a), (1, start_b)):
            piece = block_sums[which * CBLK:(which + 1) * CBLK]
            mass_piece = block_mass[which * CBLK:(which + 1) * CBLK]
            old_sums = lax.dynamic_slice_in_dim(weighted_sums, start, CBLK, 0)
            weighted_sums = lax.dynamic_update_slice_in_dim(weighted_sums, old_sums + piece, start, 0)
            old_mass = lax.dynamic_slice_in_dim(mass_total, start, CBLK, 0)
            mass_total = lax.dynamic_update_slice_in_dim(mass_total, old_mass + mass_piece, start, 0)
        return (weighted_sums, mass_total), None

    start_carry = (jnp.zeros((K1, D), jnp.float32), jnp.zeros((K1,), jnp.float32))
    (weighted_sums, mass_total), _ = lax.scan(one_block, start_carry, (point_blocks, candidates))
    level_one_next = (weighted_sums + prior_mass * level_one.astype(jnp.float32)) / (mass_total[:, None] + prior_mass)

    centres = level_one_next.reshape(K1 // CBLK, CBLK, D)
    top_float = level_two.astype(jnp.float32)
    top_squares = jnp.sum(jnp.square(top_float), 1)

    def top_block(carry, centre_rows):
        top_sums, top_mass = carry
        products = lax.dot_general(centre_rows, top_float, (((1,), (1,)), ((), ())), precision=highest, preferred_element_type=jnp.float32)
        top_scores = (2.0 * products - top_squares[None, :]) / temp_two
        top_weights = jax.nn.softmax(top_scores, axis=1)
        top_sums = top_sums + lax.dot_general(top_weights, centre_rows, (((0,), (0,)), ((), ())), precision=highest, preferred_element_type=jnp.float32)
        top_mass = top_mass + jnp.sum(top_weights, 0)
        return (top_sums, top_mass), None

    top_carry = (jnp.zeros((K2, D), jnp.float32), jnp.zeros((K2,), jnp.float32))
    (top_sums, top_mass), _ = lax.scan(top_block, top_carry, centres)
    level_two_next = (top_sums + prior_mass * top_float) / (top_mass[:, None] + prior_mass)
    return level_one_next, level_two_next
```

```python
import functools

import jax
import jax.numpy as jnp
from jax import lax
from jax.experimental import pallas as pl
from jax.experimental.pallas import tpu as pltpu
from jax.sharding import PartitionSpec as P

MESH = pl.DeviceIdType.MESH
CAP = 2
PRIOR = 1.0
BIG = 1e5
F32 = jnp.float32
BF16 = jnp.bfloat16
PEERS = [(dy, dz) for dy in range(4) for dz in range(4) if (dy, dz) != (0, 0)]
NEAR = [(dy, dz) for dy in (0, 1, 3) for dz in (0, 1, 3)]
FAR = [(2, 0), (2, 1), (2, 2), (2, 3), (0, 2), (1, 2), (3, 2)]
AXES_OF = ((2, 1, 0), (1, 0, 2), (0, 2, 1))


def nt(left, right):
    return lax.dot_general(
        left, right, (((1,), (1,)), ((), ())), preferred_element_type=F32
    )


def nn(left, right):
    return jnp.dot(left, right, preferred_element_type=F32)


def log_add(a, b):
    top = jnp.maximum(a, b)
    return top + jnp.log(jnp.exp(a - top) + jnp.exp(b - top))


def source_of(i):
    j = i - 9
    near_y, near_z = i // 3, i % 3
    far_t = j - 4
    dy = jnp.where(
        i < 9, near_y + near_y // 2, jnp.where(j < 4, 2, far_t + far_t // 2)
    )
    dz = jnp.where(i < 9, near_z + near_z // 2, jnp.where(j < 4, j, 2))
    return dy, dz


def step_kernel(
    pts, cen, table, zin,
    one_out, two_out,
    tt, tt_sib, tts, zg1, zg2, zg3, yg1, yg2, yg3, outz, outy, x_all, c_all, sq, scores,
    st, sto, stc, g_all, lse, w_buf, sums, sum_half, sum_full,
    mass, mass_in, z_all, zsq, ch, stat, stat_in, wh, wl,
    ha0, fu0, ha1, fu1, ha2, fu2,
    ssem, rsem, lsem,
):
    dp = lax.axis_index("dp")
    cent = lax.axis_index("cent")
    y, z = dp // 4, dp % 4
    x, c = cent // 2, cent % 2
    zg = (None, zg1, zg2, zg3)
    yg = (None, yg1, yg2, yg3)

    def at(dy=0, dz=0, dx=0, dc=0):
        return (
            ((y + dy) % 4) * 4 + (z + dz) % 4,
            ((x + dx) % 4) * 2 + (c + dc) % 2,
        )

    def along(axis, d):
        return at(*[d if a == axis else 0 for a in range(3)])

    sent = []
    counter = [0]

    def send(src, dst, device):
        n = counter[0]
        counter[0] += 1
        copy = pltpu.make_async_remote_copy(
            src_ref=src,
            dst_ref=dst,
            send_sem=ssem.at[n],
            recv_sem=rsem.at[n],
            device_id=device,
            device_id_type=MESH,
        )
        copy.start()
        sent.append(copy)
        return copy

    barrier = pltpu.get_barrier_semaphore()
    friends = [dict(dy=a, dz=b) for a, b in PEERS]
    friends += [dict(dc=1), dict(dx=1), dict(dx=2), dict(dx=3)]
    for f in friends:
        pl.semaphore_signal(barrier, inc=1, device_id=at(**f), device_id_type=MESH)
    pl.semaphore_wait(barrier, len(friends))

    z_one = {d: send(pts.at[:, 0], zg[d], along(1, d)) for d in (1, 3)}
    y_one = {d: send(pts.at[:, 1], yg[d], along(0, d)) for d in (1, 3)}
    c_one = {d: send(cen, c_all.at[d], along(2, d)) for d in (1, 3)}
    t_copy = {
        (a, b): send(table, tt.at[dp], at(dy=a, dz=b)) for a, b in PEERS
    }
    zx = {d: send(zin, z_all.at[0, 0, d], along(2, d)) for d in (1, 2, 3)}
    tt[dp] = table[...]
    c_all[0] = cen[...]
    z_all[0, 0, 0] = zin[...]
    for t in t_copy.values():
        t.wait_recv()
    tt_copy = send(tt, tt_sib, at(dc=1))
    local = pltpu.make_async_copy(tt, tts, lsem.at[0])
    local.start()
    local.wait()

    arrive = {}

    def slots(r):
        from_z = tts.at[y * 4 + (z - r) % 4]
        from_y = tts.at[((y - r) % 4) * 4 + z]
        for d in (2, 1, 3, 0):
            for k in range(2):
                group = ((y + d) % 4) * 4 + z
                pick = from_z[0, group * CAP + k]
                block = pts[pick, 0] if r == 0 else zg[r][pick]
                if d == 0:
                    x_all[r, k, c, 0] = block
                else:
                    outz[r, d - 1, k] = block
                group = y * 4 + (z + d) % 4
                pick = from_y[0, group * CAP + k]
                block = pts[pick, 1] if r == 0 else yg[r][pick]
                if d == 0:
                    x_all[r * 4, k, c, 1] = block
                else:
                    outy[r, d - 1, k] = block
            if d != 0:
                arrive[d, r, 0] = send(
                    outz.at[r, d - 1], x_all.at[d * 4 + r, :, c, 0], along(0, d)
                )
                arrive[r, d, 1] = send(
                    outy.at[r, d - 1], x_all.at[r * 4 + d, :, c, 1], along(1, d)
                )

    slots(0)
    z_one[1].wait_recv()
    z_fwd = [send(zg[1].at[0:4], zg[2].at[0:4], along(1, 1))]
    y_one[1].wait_recv()
    y_fwd = [send(yg[1].at[0:4], yg[2].at[0:4], along(0, 1))]
    z_one[3].wait_recv()
    z_fwd.append(send(zg[3].at[4:8], zg[2].at[4:8], along(1, 3)))
    y_one[3].wait_recv()
    y_fwd.append(send(yg[3].at[4:8], yg[2].at[4:8], along(0, 3)))
    c_one[1].wait_recv()
    c_fwd = [send(c_all.at[1, 0:128], c_all.at[2, 0:128], along(2, 1))]
    c_one[3].wait_recv()
    c_fwd.append(send(c_all.at[3, 128:256], c_all.at[2, 128:256], along(2, 3)))
    slots(1)
    slots(3)
    for copy in z_fwd + y_fwd:
        copy.wait_recv()
    slots(2)
    for copy in c_fwd:
        copy.wait_recv()

    centres = c_all[...].reshape(1024, 1024)
    sq[...] = (
        jnp.sum(jnp.square(centres.astype(F32)), 1, keepdims=True) * (1.0 / 64.0)
        + jnp.zeros((1024, 128), F32)
    )

    def score_chunk(i, carry):
        dy, dz = source_of(i)
        s = dy * 4 + dz
        s_abs = ((y - dy) % 4) * 4 + (z - dz) % 4
        rows = x_all[s].reshape(256, 1024)
        product = nt(c_all[...].reshape(1024, 1024), rows)
        for k in range(2):
            half = product[:, k * 128:(k + 1) * 128] * (1.0 / 32.0) - sq[...]
            scores[s * 2 + k] = half.reshape(4, 4, 4, 16, 128)
            peak = jnp.max(half, 0, keepdims=True)
            total = jnp.sum(jnp.exp(half - peak), 0, keepdims=True)
            st[k, pl.ds(s_abs, 1), :] = peak + jnp.log(total)
        return carry

    sib = {}

    def forward(group):
        for dy, dz in group:
            s = dy * 4 + dz
            if dy:
                arrive[dy, dz, 0].wait_recv()
            if dz:
                arrive[dy, dz, 1].wait_recv()
            sib[dy, dz] = send(x_all.at[s, :, c], x_all.at[s, :, c], at(dc=1))

    forward(NEAR)
    for p in NEAR:
        sib[p].wait_recv()
    lax.fori_loop(0, 9, score_chunk, 0)
    forward(FAR)
    for p in FAR:
        sib[p].wait_recv()
    lax.fori_loop(9, 16, score_chunk, 0)

    st_copy = send(st, sto, at(dc=1))
    st_copy.wait_recv()
    stc[...] = log_add(st[...], sto[...])
    g_copies = [send(stc, g_all.at[dp], at(dy=a, dz=b)) for a, b in PEERS]
    g_all[dp] = stc[...]
    for copy in zx.values():
        copy.wait_recv()
    for copy in g_copies:
        copy.wait_recv()
    zz = [send(z_all.at[0, 0], z_all.at[0, d], along(1, d)) for d in (1, 2, 3)]
    tt_copy.wait_recv()
    lane = lax.broadcasted_iota(jnp.int32, (16, 128), 1)
    mine = lane // 64 == c
    wide = lax.broadcasted_iota(jnp.int32, (16, 512), 1).astype(F32)
    source = lax.broadcasted_iota(jnp.int32, (16, 1), 0).astype(F32)
    table_rows = g_all[...].reshape(512, 128)

    def other_group(tables_of, k):
        partner = tables_of[:, 1, :].astype(F32)
        slot = jnp.sum(jnp.where(lane == dp * CAP + k, partner, 0.0), 1, keepdims=True)
        match = (wide == slot * 16.0 + source).astype(F32)
        other = jnp.dot(
            match, table_rows, precision=lax.Precision.HIGHEST, preferred_element_type=F32
        )
        return jnp.where(slot >= 0.0, log_add(stc[k], other), BIG)

    for k in range(2):
        lse[k] = jnp.where(mine, other_group(tt, k), other_group(tt_sib, k))

    def weigh(r):
        def one(s, carry):
            dy, dz = s // 4, s % 4
            s_abs = ((y - dy) % 4) * 4 + (z - dz) % 4
            for k in range(2):
                col = pl.multiple_of(s * 256 + k * 128, 128)
                row = lse[k, pl.ds(s_abs, 1), :]
                w_buf[:, pl.ds(col, 128)] = jnp.exp(
                    scores[s * 2 + k, r].reshape(256, 128) - row
                ).astype(BF16)
            return carry

        lax.fori_loop(0, 16, one, 0)
        mass[r] = nt(jnp.ones((8, 4096), BF16), w_buf[...])

        def tile(n, carry):
            col = pl.multiple_of(n * 256, 256)
            rows = x_all[:, :, :, :, :, pl.ds(col, 256)].reshape(4096, 256)
            sums[r, :, pl.ds(col, 256)] = nn(w_buf[...], rows)
            return carry

        lax.fori_loop(0, 4, tile, 0)

    lo, hi = pl.ds(0, 128), pl.ds(128, 128)
    weigh(2)
    via_a = send(sums.at[2, lo], sum_half.at[0], along(2, 1))
    via_b = send(sums.at[2, hi], sum_half.at[1], along(2, 3))
    mass_a = send(mass.at[2], mass_in.at[0], along(2, 1))
    for copy in zz:
        copy.wait_recv()
    zy = [send(z_all.at[0], z_all.at[d], along(0, d)) for d in (1, 2, 3)]
    weigh(3)
    last = [send(sums.at[3, hi], sum_full.at[0, hi], along(2, 1))]
    weigh(1)
    last.append(send(sums.at[1, lo], sum_full.at[1, lo], along(2, 3)))
    last.append(send(mass.at[1], mass_in.at[2], along(2, 3)))
    via_a.wait_recv()
    sums[3, lo] += sum_half[0]
    last.append(send(sums.at[3, lo], sum_full.at[0, lo], along(2, 1)))
    mass_a.wait_recv()
    mass[3] += mass_in[0]
    last.append(send(mass.at[3], mass_in.at[1], along(2, 1)))
    via_b.wait_recv()
    sums[1, hi] += sum_half[1]
    last.append(send(sums.at[1, hi], sum_full.at[1, hi], along(2, 3)))
    weigh(0)
    for copy in zy:
        copy.wait_recv()
    zsq[...] = (
        jnp.sum(
            jnp.square(z_all[...].reshape(1024, 1024).astype(F32)), 1, keepdims=True
        ) * (1.0 / 16.0)
        + jnp.zeros((1024, 128), F32)
    )
    for copy in last:
        copy.wait_recv()
    own_mass = jnp.transpose(mass[0] + mass_in[1] + mass_in[2])[:, 0:1]
    own_sums = sums[0] + sum_full[0] + sum_full[1]
    one_out[...] = (own_sums + PRIOR * cen[...].astype(F32)) / (own_mass + PRIOR)

    ch[0, 0] = one_out[...].astype(BF16)
    ch[0, 1] = (one_out[...] - ch[0, 0].astype(F32)).astype(BF16)
    ch_copy = send(ch.at[0], ch.at[1], at(dc=1))

    def top_scores(h, carry):
        zs = z_all[...].reshape(1024, 1024)
        product = nt(zs, ch[h, 0]) + nt(zs, ch[h, 1])
        for k in range(2):
            cols = slice(k * 128, (k + 1) * 128)
            half = product[:, cols] * (1.0 / 8.0) - zsq[...]
            scores[16 + h * 2 + k] = half.reshape(4, 4, 4, 16, 128)
            peak = jnp.max(half, 0, keepdims=True)
            stat[h, 0:1, cols] = peak
            stat[h, 1:2, cols] = jnp.sum(jnp.exp(half - peak), 0, keepdims=True)
        return carry

    lax.fori_loop(0, 1, top_scores, 0)
    ch_copy.wait_recv()
    lax.fori_loop(1, 2, top_scores, 0)
    stat_copy = send(stat, stat_in, at(dc=1))
    stat_copy.wait_recv()
    mass_two = jnp.zeros((1024, 1), F32)
    for h in range(2):
        peak = jnp.maximum(stat[h, 0:1], stat_in[1 - h, 0:1])
        total = stat[h, 1:2] * jnp.exp(stat[h, 0:1] - peak) + stat_in[
            1 - h, 1:2
        ] * jnp.exp(stat_in[1 - h, 0:1] - peak)
        scale = 1.0 / total
        for k in range(2):
            part = slice(k * 128, (k + 1) * 128)
            weight = (
                jnp.exp(scores[16 + h * 2 + k].reshape(1024, 128) - peak[:, part])
                * scale[:, part]
            )
            cols = slice(h * 256 + k * 128, h * 256 + (k + 1) * 128)
            wh[:, cols] = weight.astype(BF16)
            wl[:, cols] = (weight - wh[:, cols].astype(F32)).astype(BF16)
            mass_two = mass_two + jnp.sum(weight, 1, keepdims=True)
    for q in range(4):
        cols = slice(q * 256, (q + 1) * 256)
        hi_rows = ch[:, 0, :, cols].reshape(512, 256)
        lo_rows = ch[:, 1, :, cols].reshape(512, 256)
        part = nn(wh[...], hi_rows) + nn(wl[...], hi_rows) + nn(wh[...], lo_rows)
        for k in range(2):
            scores[q * 2 + k] = part[:, k * 128:(k + 1) * 128].reshape(4, 4, 4, 16, 128)
    scores[8] = (mass_two + jnp.zeros((1024, 128), F32)).reshape(4, 4, 4, 16, 128)

    halves = (ha0, ha1, ha2)
    fulls = (fu0, fu1, fu2)

    def chunk(q, stage, r, half=None):
        where = [slice(None)] * 3
        for done in AXES_OF[q][:stage]:
            where[done] = 0
        where[AXES_OF[q][stage]] = r
        if half is not None:
            if stage < 2:
                free = min(AXES_OF[q][stage + 1:])
                where[free] = pl.ds(half * 2, 2)
            else:
                where.append(pl.ds(half * 8, 8))
        return scores.at[(pl.ds(q * 3, 3), *where)]

    def part_of(ref, stage, half):
        size = 2 if stage < 2 else 8
        return ref.at[:, pl.ds(half * size, size)]

    for stage in range(3):
        ha, fu = halves[stage], fulls[stage]
        first, second = {}, {}
        for q in range(3):
            axis = AXES_OF[q][stage]
            first[q] = (
                send(chunk(q, stage, 2, 0), ha.at[q, 0], along(axis, 1)),
                send(chunk(q, stage, 2, 1), ha.at[q, 1], along(axis, 3)),
            )
        for q in range(3):
            axis = AXES_OF[q][stage]
            second[q] = [
                send(chunk(q, stage, 3, 1), part_of(fu.at[q, 0], stage, 1), along(axis, 1)),
                send(chunk(q, stage, 1, 0), part_of(fu.at[q, 1], stage, 0), along(axis, 3)),
            ]
        for q in range(3):
            axis = AXES_OF[q][stage]
            first[q][0].wait_recv()
            view = chunk(q, stage, 3, 0)
            view[...] += ha[q, 0]
            second[q].append(send(view, part_of(fu.at[q, 0], stage, 0), along(axis, 1)))
            first[q][1].wait_recv()
            view = chunk(q, stage, 1, 1)
            view[...] += ha[q, 1]
            second[q].append(send(view, part_of(fu.at[q, 1], stage, 1), along(axis, 3)))
        for q in range(3):
            for copy in second[q]:
                copy.wait_recv()
            view = chunk(q, stage, 0)
            view[...] += fu[q, 0] + fu[q, 1]
    denominator = scores[8, 0, 0, 0, :, 0:1] + PRIOR
    for q in range(8):
        cols = slice(q * 128, (q + 1) * 128)
        two_out[:, cols] = (
            scores[q, 0, 0, 0] + PRIOR * zin[:, cols].astype(F32)
        ) / denominator
    for copy in sent:
        copy.wait_send()


def tables(candidates):
    targets = candidates.reshape(-1)
    count = targets.shape[0]
    position = jnp.arange(count, dtype=jnp.int32)
    earlier = (targets[None, :] == targets[:, None]) & (
        position[None, :] < position[:, None]
    )
    slot = targets * CAP + jnp.sum(earlier.astype(jnp.int32), 1)
    mate = jnp.stack([slot[1::2], slot[0::2]], 1).reshape(-1)
    lanes = jnp.arange(128, dtype=jnp.int32)
    hit = slot[:, None] == lanes[None, :]
    block = jnp.sum(jnp.where(hit, (position // 2)[:, None], 0), 0)
    partner = jnp.sum(jnp.where(hit, mate[:, None] + 1, 0), 0) - 1
    rest = jnp.zeros((6, 128), jnp.int32)
    return jnp.concatenate([block[None], partner[None], rest], 0)


def local(points, candidates, level_one, level_two):
    vmem = pl.BlockSpec(memory_space=pltpu.VMEM)
    n_copies = 158
    dma = pltpu.SemaphoreType.DMA
    scratch = [
        pltpu.VMEM((16, 8, 128), jnp.int32),
        pltpu.VMEM((16, 8, 128), jnp.int32),
        pltpu.SMEM((16, 8, 128), jnp.int32),
        *[pltpu.VMEM((8, 32, 1024), BF16)] * 3,
        *[pltpu.VMEM((8, 32, 1024), BF16)] * 3,
        pltpu.VMEM((4, 3, 2, 32, 1024), BF16),
        pltpu.VMEM((4, 3, 2, 32, 1024), BF16),
        pltpu.VMEM((16, 2, 2, 2, 32, 1024), BF16),
        pltpu.VMEM((4, 256, 1024), BF16),
        pltpu.VMEM((1024, 128), F32),
        pltpu.VMEM((32, 4, 4, 4, 16, 128), F32),
        pltpu.VMEM((2, 16, 128), F32),
        pltpu.VMEM((2, 16, 128), F32),
        pltpu.VMEM((2, 16, 128), F32),
        pltpu.VMEM((16, 2, 16, 128), F32),
        pltpu.VMEM((2, 16, 128), F32),
        pltpu.VMEM((256, 4096), BF16),
        pltpu.VMEM((4, 256, 1024), F32),
        pltpu.VMEM((2, 128, 1024), F32),
        pltpu.VMEM((2, 256, 1024), F32),
        pltpu.VMEM((4, 8, 256), F32),
        pltpu.VMEM((3, 8, 256), F32),
        pltpu.VMEM((4, 4, 4, 16, 1024), BF16),
        pltpu.VMEM((1024, 128), F32),
        pltpu.VMEM((2, 2, 256, 1024), BF16),
        pltpu.VMEM((2, 8, 256), F32),
        pltpu.VMEM((2, 8, 256), F32),
        pltpu.VMEM((1024, 512), BF16),
        pltpu.VMEM((1024, 512), BF16),
        pltpu.VMEM((3, 2, 3, 2, 4, 16, 128), F32),
        pltpu.VMEM((3, 2, 3, 4, 4, 16, 128), F32),
        pltpu.VMEM((3, 2, 3, 2, 16, 128), F32),
        pltpu.VMEM((3, 2, 3, 4, 16, 128), F32),
        pltpu.VMEM((3, 2, 3, 8, 128), F32),
        pltpu.VMEM((3, 2, 3, 16, 128), F32),
        dma((n_copies,)),
        dma((n_copies,)),
        dma((1,)),
    ]
    return pl.pallas_call(
        step_kernel,
        out_shape=(
            jax.ShapeDtypeStruct((256, 1024), F32),
            jax.ShapeDtypeStruct((16, 1024), F32),
        ),
        in_specs=[vmem] * 4,
        out_specs=(vmem, vmem),
        scratch_shapes=scratch,
        compiler_params=pltpu.CompilerParams(
            collective_id=0, has_side_effects=True, vmem_limit_bytes=62 * 2**20
        ),
        name="lloyd_step",
    )(points.reshape(8, 2, 32, 1024), level_one, tables(candidates), level_two)


def solution(mesh):
    placed = P(("dp", "cent"), None)
    return jax.shard_map(
        local,
        mesh=mesh,
        in_specs=(placed,) * 4,
        out_specs=(placed, placed),
        check_vma=False,
    )
```

```python
import functools

import jax
import jax.numpy as jnp
from jax import lax
from jax.experimental import pallas as pl
from jax.experimental.pallas import tpu as pltpu
from jax.sharding import PartitionSpec as P

MESH = pl.DeviceIdType.MESH
CAP = 2
PRIOR = 1.0
BIG = 1e5
LIMIT = 32767.0
F32 = jnp.float32
BF16 = jnp.bfloat16
PEERS = [(dy, dz) for dy in range(4) for dz in range(4) if (dy, dz) != (0, 0)]
ORDER = [(0, 0), (0, 1), (1, 0), (0, 3), (3, 0), (1, 1), (1, 3), (3, 1), (3, 3)]
ORDER += [(2, 0), (0, 2), (2, 1), (1, 2), (2, 3), (3, 2), (2, 2)]
AXES_OF = ((2, 1, 0), (1, 0, 2), (0, 2, 1))


def nt(left, right):
    return lax.dot_general(
        left, right, (((1,), (1,)), ((), ())), preferred_element_type=F32
    )


def nn(left, right):
    return jnp.dot(left, right, preferred_element_type=F32)


def log_add(a, b):
    top = jnp.maximum(a, b)
    return top + jnp.log(jnp.exp(a - top) + jnp.exp(b - top))


def encode(value, code, scale, row):
    peak = jnp.maximum(jnp.max(jnp.abs(value), 1, keepdims=True), 1e-30)
    code[...] = jnp.round(value * (LIMIT / peak)).astype(jnp.int32).astype(jnp.int16)
    wide = peak * (1.0 / LIMIT) + jnp.zeros((128, 128), F32)
    scale[row:row + 1, :] = jnp.transpose(wide)[0:1, :]


def decode(code, scale, row):
    wide = jnp.transpose(scale[...])
    return code[...].astype(jnp.int32).astype(F32) * wide[:, row:row + 1]


def source_of(i):
    code = sum(jnp.where(i == n, dy * 4 + dz, 0) for n, (dy, dz) in enumerate(ORDER))
    return code // 4, code % 4


def step_kernel(
    pts, cen, table, own, zin,
    one_out, two_out,
    tt, tt_sib, tts, zg1, zg2, zg3, yg1, yg2, yg3, outz, outy, x_all, c_all, sq, scores,
    st, sto, stc, g_all, peaks, alpha, w_buf, sums, code_out, code_in, scale_out, scale_in,
    mass, mass_in, z_all, zsq, ch, stat, stat_in, wh, wl,
    t_code, t_code_in, t_scale, t_scale_in, ha1, fu1, ha2, fu2,
    ssem, rsem, lsem,
):
    dp = lax.axis_index("dp")
    cent = lax.axis_index("cent")
    y, z = dp // 4, dp % 4
    x, c = cent // 2, cent % 2
    zg = (None, zg1, zg2, zg3)
    yg = (None, yg1, yg2, yg3)

    def at(dy=0, dz=0, dx=0, dc=0):
        return (
            ((y + dy) % 4) * 4 + (z + dz) % 4,
            ((x + dx) % 4) * 2 + (c + dc) % 2,
        )

    def along(axis, d):
        return at(*[d if a == axis else 0 for a in range(3)])

    sent = []
    counter = [0]

    def send(src, dst, device):
        n = counter[0]
        counter[0] += 1
        copy = pltpu.make_async_remote_copy(
            src_ref=src,
            dst_ref=dst,
            send_sem=ssem.at[n],
            recv_sem=rsem.at[n],
            device_id=device,
            device_id_type=MESH,
        )
        copy.start()
        sent.append(copy)
        return copy

    barrier = pltpu.get_barrier_semaphore()
    friends = [dict(dy=a, dz=b) for a, b in PEERS]
    friends += [dict(dc=1), dict(dx=1), dict(dx=2), dict(dx=3)]
    for f in friends:
        pl.semaphore_signal(barrier, inc=1, device_id=at(**f), device_id_type=MESH)
    pl.semaphore_wait(barrier, len(friends))

    t_near, t_far = [], []
    for d in (1, 2, 3):
        t_near.append(send(table, tt.at[dp], along(1, d)))
        t_near.append(send(table, tt.at[dp], along(0, d)))
    z_one = {d: send(pts.at[:, 0], zg[d], along(1, d)) for d in (1, 3)}
    y_one = {d: send(pts.at[:, 1], yg[d], along(0, d)) for d in (1, 3)}
    c_one = {d: send(cen, c_all.at[d], along(2, d)) for d in (1, 3)}
    tt[dp] = table[...]
    c_all[0] = cen[...]
    z_all[0, 0, 0] = zin[...]

    arrive = {}

    def slots(r):
        from_z = own if r == 0 else tts.at[y * 4 + (z - r) % 4]
        from_y = own if r == 0 else tts.at[((y - r) % 4) * 4 + z]
        for d in (2, 1, 3, 0):
            for k in range(2):
                group = ((y + d) % 4) * 4 + z
                pick = from_z[0, group * CAP + k]
                block = pts[pick, 0] if r == 0 else zg[r][pick]
                if d == 0:
                    x_all[r, k, c, 0] = block
                else:
                    outz[r, d - 1, k] = block
                group = y * 4 + (z + d) % 4
                pick = from_y[0, group * CAP + k]
                block = pts[pick, 1] if r == 0 else yg[r][pick]
                if d == 0:
                    x_all[r * 4, k, c, 1] = block
                else:
                    outy[r, d - 1, k] = block
            if d != 0:
                arrive[d, r, 0] = send(
                    outz.at[r, d - 1], x_all.at[d * 4 + r, :, c, 0], along(0, d)
                )
                arrive[r, d, 1] = send(
                    outy.at[r, d - 1], x_all.at[r * 4 + d, :, c, 1], along(1, d)
                )

    slots(0)
    for a, b in PEERS:
        if a and b:
            t_far.append(send(table, tt.at[dp], at(dy=a, dz=b)))
    zx = {d: send(zin, z_all.at[0, 0, d], along(2, d)) for d in (1, 2, 3)}
    for t in t_near + t_far:
        t.wait_recv()
    tt_copy = send(tt, tt_sib, at(dc=1))
    local = pltpu.make_async_copy(tt, tts, lsem.at[0])
    local.start()
    local.wait()
    z_one[1].wait_recv()
    z_fwd = [send(zg[1].at[0:4], zg[2].at[0:4], along(1, 1))]
    y_one[1].wait_recv()
    y_fwd = [send(yg[1].at[0:4], yg[2].at[0:4], along(0, 1))]
    z_one[3].wait_recv()
    z_fwd.append(send(zg[3].at[4:8], zg[2].at[4:8], along(1, 3)))
    y_one[3].wait_recv()
    y_fwd.append(send(yg[3].at[4:8], yg[2].at[4:8], along(0, 3)))
    c_one[1].wait_recv()
    c_fwd = [send(c_all.at[1, 0:128], c_all.at[2, 0:128], along(2, 1))]
    c_one[3].wait_recv()
    c_fwd.append(send(c_all.at[3, 128:256], c_all.at[2, 128:256], along(2, 3)))
    slots(1)
    slots(3)
    for copy in z_fwd + y_fwd:
        copy.wait_recv()
    slots(2)
    for copy in c_fwd:
        copy.wait_recv()

    centres = c_all[...].reshape(1024, 1024)
    sq[...] = (
        jnp.sum(jnp.square(centres.astype(F32)), 1, keepdims=True) * (1.0 / 64.0)
        + jnp.zeros((1024, 128), F32)
    )

    def score_chunk(i, carry):
        dy, dz = source_of(i)
        s = dy * 4 + dz
        s_abs = ((y - dy) % 4) * 4 + (z - dz) % 4
        rows = x_all[s].reshape(256, 1024)
        product = nt(c_all[...].reshape(1024, 1024), rows)
        for k in range(2):
            half = product[:, k * 128:(k + 1) * 128] * (1.0 / 32.0) - sq[...]
            peak = jnp.max(half, 0, keepdims=True)
            raised = jnp.exp(half - peak)
            scores[s * 2 + k] = raised.reshape(4, 4, 4, 16, 128)
            total = jnp.sum(raised, 0, keepdims=True)
            peaks[k, pl.ds(s_abs, 1), :] = peak
            st[k, pl.ds(s_abs, 1), :] = peak + jnp.log(total)
        return carry

    sib = {}

    def forward(group):
        for dy, dz in group:
            s = dy * 4 + dz
            if dy:
                arrive[dy, dz, 0].wait_recv()
            if dz:
                arrive[dy, dz, 1].wait_recv()
            sib[dy, dz] = send(x_all.at[s, :, c], x_all.at[s, :, c], at(dc=1))

    def score(lo, hi):
        for p in ORDER[lo:hi]:
            sib[p].wait_recv()
        lax.fori_loop(lo, hi, score_chunk, 0)

    forward(ORDER[0:5])
    forward(ORDER[5:9])
    score(0, 5)
    forward(ORDER[9:11])
    score(5, 9)
    forward(ORDER[11:15])
    score(9, 11)
    score(11, 14)
    forward(ORDER[15:])
    score(14, 15)
    score(15, 16)

    st_copy = send(st, sto, at(dc=1))
    st_copy.wait_recv()
    stc[...] = log_add(st[...], sto[...])
    g_copies = [send(stc, g_all.at[dp], at(dy=a, dz=b)) for a, b in PEERS]
    g_all[dp] = stc[...]
    for copy in zx.values():
        copy.wait_recv()
    for copy in g_copies:
        copy.wait_recv()
    zz = [send(z_all.at[0, 0], z_all.at[0, d], along(1, d)) for d in (1, 2, 3)]
    tt_copy.wait_recv()
    lane = lax.broadcasted_iota(jnp.int32, (16, 128), 1)
    mine = lane // 64 == c
    wide = lax.broadcasted_iota(jnp.int32, (16, 512), 1).astype(F32)
    source = lax.broadcasted_iota(jnp.int32, (16, 1), 0).astype(F32)
    table_rows = g_all[...].reshape(512, 128)

    def other_group(tables_of, k):
        partner = tables_of[:, 1, :].astype(F32)
        slot = jnp.sum(jnp.where(lane == dp * CAP + k, partner, 0.0), 1, keepdims=True)
        match = (wide == slot * 16.0 + source).astype(F32)
        other = jnp.dot(
            match, table_rows, precision=lax.Precision.HIGHEST, preferred_element_type=F32
        )
        return jnp.where(slot >= 0.0, log_add(stc[k], other), BIG)

    for k in range(2):
        total = jnp.where(mine, other_group(tt, k), other_group(tt_sib, k))
        alpha[k] = jnp.exp(peaks[k] - total)

    def weigh(r):
        def one(s, carry):
            dy, dz = s // 4, s % 4
            s_abs = ((y - dy) % 4) * 4 + (z - dz) % 4
            for k in range(2):
                col = pl.multiple_of(s * 256 + k * 128, 128)
                row = alpha[k, pl.ds(s_abs, 1), :]
                w_buf[:, pl.ds(col, 128)] = (
                    scores[s * 2 + k, r].reshape(256, 128) * row
                ).astype(BF16)
            return carry

        lax.fori_loop(0, 16, one, 0)
        mass[r] = nt(jnp.ones((8, 4096), BF16), w_buf[...])

        def tile(n, carry):
            col = pl.multiple_of(n * 256, 256)
            rows = x_all[:, :, :, :, :, pl.ds(col, 256)].reshape(4096, 256)
            sums[r, :, pl.ds(col, 256)] = nn(w_buf[...], rows)
            return carry

        lax.fori_loop(0, 4, tile, 0)

    lo, hi = slice(0, 128), slice(128, 256)

    def push(n, value, d):
        encode(value, code_out.at[n], scale_out.at[n], 0)
        return (
            send(code_out.at[n], code_in.at[n], along(2, d)),
            send(scale_out.at[n], scale_in.at[n], along(2, d)),
        )

    def pull(n, copies):
        for copy in copies:
            copy.wait_recv()
        return decode(code_in.at[n], scale_in.at[n], 0)

    weigh(2)
    via_a = push(0, sums[2, lo], 1)
    via_b = push(1, sums[2, hi], 3)
    mass_a = send(mass.at[2], mass_in.at[0], along(2, 1))
    for copy in zz:
        copy.wait_recv()
    zy = [send(z_all.at[0], z_all.at[d], along(0, d)) for d in (1, 2, 3)]
    weigh(3)
    up_hi = push(3, sums[3, hi], 1)
    weigh(1)
    down_lo = push(4, sums[1, lo], 3)
    mass_down = send(mass.at[1], mass_in.at[2], along(2, 3))
    up_lo = push(2, sums[3, lo] + pull(0, via_a), 1)
    mass_a.wait_recv()
    mass[3] += mass_in[0]
    mass_up = send(mass.at[3], mass_in.at[1], along(2, 1))
    down_hi = push(5, sums[1, hi] + pull(1, via_b), 3)
    weigh(0)
    for copy in zy:
        copy.wait_recv()
    zsq[...] = (
        jnp.sum(
            jnp.square(z_all[...].reshape(1024, 1024).astype(F32)), 1, keepdims=True
        ) * (1.0 / 16.0)
        + jnp.zeros((1024, 128), F32)
    )
    mass_down.wait_recv()
    mass_up.wait_recv()
    own_mass = jnp.transpose(mass[0] + mass_in[1] + mass_in[2])[:, 0:1]
    for rows, above, n_above, below, n_below in (
        (hi, up_hi, 3, down_hi, 5),
        (lo, up_lo, 2, down_lo, 4),
    ):
        total = sums[0, rows] + pull(n_above, above) + pull(n_below, below)
        one_out[rows] = (total + PRIOR * cen[rows].astype(F32)) / (
            own_mass[rows] + PRIOR
        )

    ch[0, 0] = one_out[...].astype(BF16)
    ch[0, 1] = (one_out[...] - ch[0, 0].astype(F32)).astype(BF16)
    ch_copy = send(ch.at[0], ch.at[1], at(dc=1))

    def top_scores(h, carry):
        zs = z_all[...].reshape(1024, 1024)
        product = nt(zs, ch[h, 0]) + nt(zs, ch[h, 1])
        for k in range(2):
            cols = slice(k * 128, (k + 1) * 128)
            half = product[:, cols] * (1.0 / 8.0) - zsq[...]
            peak = jnp.max(half, 0, keepdims=True)
            raised = jnp.exp(half - peak)
            scores[16 + h * 2 + k] = raised.reshape(4, 4, 4, 16, 128)
            stat[h, 0:1, cols] = peak
            stat[h, 1:2, cols] = jnp.sum(raised, 0, keepdims=True)
        return carry

    lax.fori_loop(0, 1, top_scores, 0)
    ch_copy.wait_recv()
    lax.fori_loop(1, 2, top_scores, 0)
    stat_copy = send(stat, stat_in, at(dc=1))
    stat_copy.wait_recv()
    mass_two = jnp.zeros((1024, 1), F32)
    for h in range(2):
        peak = jnp.maximum(stat[h, 0:1], stat_in[1 - h, 0:1])
        mine_up = jnp.exp(stat[h, 0:1] - peak)
        total = stat[h, 1:2] * mine_up + stat_in[1 - h, 1:2] * jnp.exp(
            stat_in[1 - h, 0:1] - peak
        )
        scale = mine_up / total
        for k in range(2):
            part = slice(k * 128, (k + 1) * 128)
            weight = (
                scores[16 + h * 2 + k].reshape(1024, 128) * scale[:, part]
            )
            cols = slice(h * 256 + k * 128, h * 256 + (k + 1) * 128)
            wh[:, cols] = weight.astype(BF16)
            wl[:, cols] = (weight - wh[:, cols].astype(F32)).astype(BF16)
            mass_two = mass_two + jnp.sum(weight, 1, keepdims=True)
    for q in range(4):
        cols = slice(q * 256, (q + 1) * 256)
        hi_rows = ch[:, 0, :, cols].reshape(512, 256)
        lo_rows = ch[:, 1, :, cols].reshape(512, 256)
        part = nn(wh[...], hi_rows) + nn(wl[...], hi_rows) + nn(wh[...], lo_rows)
        for k in range(2):
            scores[q * 2 + k] = part[:, k * 128:(k + 1) * 128].reshape(4, 4, 4, 16, 128)
    scores[8] = (mass_two + jnp.zeros((1024, 128), F32)).reshape(4, 4, 4, 16, 128)

    halves = (None, ha1, ha2)
    fulls = (None, fu1, fu2)

    def chunk(q, stage, r, half=None):
        where = [slice(None)] * 3
        for done in AXES_OF[q][:stage]:
            where[done] = 0
        where[AXES_OF[q][stage]] = r
        if half is not None:
            if stage < 2:
                free = min(AXES_OF[q][stage + 1:])
                where[free] = pl.ds(half * 2, 2)
            else:
                where.append(pl.ds(half * 8, 8))
        return scores.at[(pl.ds(q * 3, 3), *where)]

    def part_of(ref, stage, half):
        size = 2 if stage < 2 else 8
        return ref.at[:, pl.ds(half * size, size)]

    def top_push(q, n, r, half, d):
        axis = AXES_OF[q][0]
        value = chunk(q, 0, r, half)[...].reshape(3, 128, 128)
        for b in range(3):
            encode(value[b], t_code.at[q, n, b], t_scale.at[q, n], b)
        return (
            send(t_code.at[q, n], t_code_in.at[q, n], along(axis, d)),
            send(t_scale.at[q, n], t_scale_in.at[q, n], along(axis, d)),
        )

    def top_pull(q, n, copies, r, half):
        for copy in copies:
            copy.wait_recv()
        view = chunk(q, 0, r, half)
        parts = [
            decode(t_code_in.at[q, n, b], t_scale_in.at[q, n], b)[None] for b in range(3)
        ]
        view[...] += jnp.concatenate(parts, 0).reshape(view.shape)

    via = [(top_push(q, 0, 2, 0, 1), top_push(q, 1, 2, 1, 3)) for q in range(3)]
    early = [(top_push(q, 3, 3, 1, 1), top_push(q, 4, 1, 0, 3)) for q in range(3)]
    late = []
    for q in range(3):
        top_pull(q, 0, via[q][0], 3, 0)
        up = top_push(q, 2, 3, 0, 1)
        top_pull(q, 1, via[q][1], 1, 1)
        late.append((up, top_push(q, 5, 1, 1, 3)))
    for q in range(3):
        top_pull(q, 3, early[q][0], 0, 1)
        top_pull(q, 4, early[q][1], 0, 0)
        top_pull(q, 2, late[q][0], 0, 0)
        top_pull(q, 5, late[q][1], 0, 1)

    for stage in range(1, 3):
        ha, fu = halves[stage], fulls[stage]
        first, second = {}, {}
        for q in range(3):
            axis = AXES_OF[q][stage]
            first[q] = (
                send(chunk(q, stage, 2, 0), ha.at[q, 0], along(axis, 1)),
                send(chunk(q, stage, 2, 1), ha.at[q, 1], along(axis, 3)),
            )
        for q in range(3):
            axis = AXES_OF[q][stage]
            second[q] = [
                send(chunk(q, stage, 3, 1), part_of(fu.at[q, 0], stage, 1), along(axis, 1)),
                send(chunk(q, stage, 1, 0), part_of(fu.at[q, 1], stage, 0), along(axis, 3)),
            ]
        for q in range(3):
            axis = AXES_OF[q][stage]
            first[q][0].wait_recv()
            view = chunk(q, stage, 3, 0)
            view[...] += ha[q, 0]
            second[q].append(send(view, part_of(fu.at[q, 0], stage, 0), along(axis, 1)))
            first[q][1].wait_recv()
            view = chunk(q, stage, 1, 1)
            view[...] += ha[q, 1]
            second[q].append(send(view, part_of(fu.at[q, 1], stage, 1), along(axis, 3)))
        for q in range(3):
            for copy in second[q]:
                copy.wait_recv()
            view = chunk(q, stage, 0)
            view[...] += fu[q, 0] + fu[q, 1]
    denominator = scores[8, 0, 0, 0, :, 0:1] + PRIOR
    for q in range(8):
        cols = slice(q * 128, (q + 1) * 128)
        two_out[:, cols] = (
            scores[q, 0, 0, 0] + PRIOR * zin[:, cols].astype(F32)
        ) / denominator
    assert counter[0] <= ssem.shape[0]
    for copy in sent:
        copy.wait_send()


def tables(candidates):
    targets = candidates.reshape(-1)
    count = targets.shape[0]
    position = jnp.arange(count, dtype=jnp.int32)
    earlier = (targets[None, :] == targets[:, None]) & (
        position[None, :] < position[:, None]
    )
    slot = targets * CAP + jnp.sum(earlier.astype(jnp.int32), 1)
    mate = jnp.stack([slot[1::2], slot[0::2]], 1).reshape(-1)
    lanes = jnp.arange(128, dtype=jnp.int32)
    hit = slot[:, None] == lanes[None, :]
    block = jnp.sum(jnp.where(hit, (position // 2)[:, None], 0), 0)
    partner = jnp.sum(jnp.where(hit, mate[:, None] + 1, 0), 0) - 1
    rest = jnp.zeros((6, 128), jnp.int32)
    return jnp.concatenate([block[None], partner[None], rest], 0)


def local(points, candidates, level_one, level_two):
    vmem = pl.BlockSpec(memory_space=pltpu.VMEM)
    n_copies = 190
    dma = pltpu.SemaphoreType.DMA
    scratch = [
        pltpu.VMEM((16, 8, 128), jnp.int32),
        pltpu.VMEM((16, 8, 128), jnp.int32),
        pltpu.SMEM((16, 8, 128), jnp.int32),
        *[pltpu.VMEM((8, 32, 1024), BF16)] * 3,
        *[pltpu.VMEM((8, 32, 1024), BF16)] * 3,
        pltpu.VMEM((4, 3, 2, 32, 1024), BF16),
        pltpu.VMEM((4, 3, 2, 32, 1024), BF16),
        pltpu.VMEM((16, 2, 2, 2, 32, 1024), BF16),
        pltpu.VMEM((4, 256, 1024), BF16),
        pltpu.VMEM((1024, 128), F32),
        pltpu.VMEM((32, 4, 4, 4, 16, 128), F32),
        pltpu.VMEM((2, 16, 128), F32),
        pltpu.VMEM((2, 16, 128), F32),
        pltpu.VMEM((2, 16, 128), F32),
        pltpu.VMEM((16, 2, 16, 128), F32),
        pltpu.VMEM((2, 16, 128), F32),
        pltpu.VMEM((2, 16, 128), F32),
        pltpu.VMEM((256, 4096), BF16),
        pltpu.VMEM((4, 256, 1024), F32),
        *[pltpu.VMEM((6, 128, 1024), jnp.int16)] * 2,
        *[pltpu.VMEM((6, 8, 128), F32)] * 2,
        pltpu.VMEM((4, 8, 256), F32),
        pltpu.VMEM((3, 8, 256), F32),
        pltpu.VMEM((4, 4, 4, 16, 1024), BF16),
        pltpu.VMEM((1024, 128), F32),
        pltpu.VMEM((2, 2, 256, 1024), BF16),
        pltpu.VMEM((2, 8, 256), F32),
        pltpu.VMEM((2, 8, 256), F32),
        pltpu.VMEM((1024, 512), BF16),
        pltpu.VMEM((1024, 512), BF16),
        *[pltpu.VMEM((3, 6, 3, 128, 128), jnp.int16)] * 2,
        *[pltpu.VMEM((3, 6, 8, 128), F32)] * 2,
        pltpu.VMEM((3, 2, 3, 2, 16, 128), F32),
        pltpu.VMEM((3, 2, 3, 4, 16, 128), F32),
        pltpu.VMEM((3, 2, 3, 8, 128), F32),
        pltpu.VMEM((3, 2, 3, 16, 128), F32),
        dma((n_copies,)),
        dma((n_copies,)),
        dma((1,)),
    ]
    table = tables(candidates)
    return pl.pallas_call(
        step_kernel,
        out_shape=(
            jax.ShapeDtypeStruct((256, 1024), F32),
            jax.ShapeDtypeStruct((16, 1024), F32),
        ),
        in_specs=[vmem, vmem, vmem, pl.BlockSpec(memory_space=pltpu.SMEM), vmem],
        out_specs=(vmem, vmem),
        scratch_shapes=scratch,
        compiler_params=pltpu.CompilerParams(
            collective_id=0, has_side_effects=True, vmem_limit_bytes=62 * 2**20
        ),
        name="lloyd_step",
    )(points.reshape(8, 2, 32, 1024), level_one, table, table, level_two)


def solution(mesh):
    placed = P(("dp", "cent"), None)
    return jax.shard_map(
        local,
        mesh=mesh,
        in_specs=(placed,) * 4,
        out_specs=(placed, placed),
        check_vma=False,
    )
```

```python
import functools

import jax
import jax.numpy as jnp
from jax import lax
from jax.experimental import pallas as pl
from jax.experimental.pallas import tpu as pltpu
from jax.sharding import PartitionSpec as P

MESH = pl.DeviceIdType.MESH
CAP = 2
PRIOR = 1.0
BIG = 1e5
LIMIT = 32767.0
F32 = jnp.float32
BF16 = jnp.bfloat16
PEERS = [(dy, dz) for dy in range(4) for dz in range(4) if (dy, dz) != (0, 0)]
ORDER = [(0, 0), (0, 1), (1, 0), (0, 3), (3, 0), (1, 1), (1, 3), (3, 1), (3, 3)]
ORDER += [(2, 0), (0, 2), (2, 1), (1, 2), (2, 3), (3, 2), (2, 2)]
AXES_OF = ((2, 1, 0), (1, 0, 2), (0, 2, 1))


def nt(left, right):
    return lax.dot_general(
        left, right, (((1,), (1,)), ((), ())), preferred_element_type=F32
    )


def nn(left, right):
    return jnp.dot(left, right, preferred_element_type=F32)


def log_add(a, b):
    top = jnp.maximum(a, b)
    return top + jnp.log(jnp.exp(a - top) + jnp.exp(b - top))


def encode(values, codes, scale):
    lane = lax.broadcasted_iota(jnp.int32, (128, 128), 1)
    wide = jnp.zeros((128, 128), F32)
    for n, (value, code) in enumerate(zip(values, codes)):
        peak = jnp.maximum(jnp.max(jnp.abs(value), 1, keepdims=True), 1e-30)
        code[...] = jnp.round(value * (LIMIT / peak)).astype(jnp.int32).astype(jnp.int16)
        wide = jnp.where(lane == n, peak * (1.0 / LIMIT), wide)
    scale[...] = jnp.transpose(wide)[0:8, :]


def decode(codes, scale):
    wide = jnp.transpose(scale[...])
    return [
        code[...].astype(jnp.int32).astype(F32) * wide[:, n:n + 1]
        for n, code in enumerate(codes)
    ]


def source_of(i):
    code = sum(jnp.where(i == n, dy * 4 + dz, 0) for n, (dy, dz) in enumerate(ORDER))
    return code // 4, code % 4


def step_kernel(
    pts, cen, table, own, zin,
    one_out, den_out, two_out,
    tt, tt_sib, tts, zg1, zg2, zg3, yg1, yg2, yg3, outz, outy, x_all, c_all, sq, scores,
    st, sto, stc, g_all, peaks, alpha, w_buf, sums, code_out, code_in, scale_out, scale_in,
    mass, mass_in, z_all, zsq, ch, stat, stat_in, wh, wl,
    t_code, t_code_in, t_scale, t_scale_in, ha1, fu1, ha2, fu2,
    ssem, rsem, lsem,
):
    dp = lax.axis_index("dp")
    cent = lax.axis_index("cent")
    y, z = dp // 4, dp % 4
    x, c = cent // 2, cent % 2
    zg = (None, zg1, zg2, zg3)
    yg = (None, yg1, yg2, yg3)

    def at(dy=0, dz=0, dx=0, dc=0):
        return (
            ((y + dy) % 4) * 4 + (z + dz) % 4,
            ((x + dx) % 4) * 2 + (c + dc) % 2,
        )

    def along(axis, d):
        return at(*[d if a == axis else 0 for a in range(3)])

    sent = []
    counter = [0]

    def send(src, dst, device):
        n = counter[0]
        counter[0] += 1
        copy = pltpu.make_async_remote_copy(
            src_ref=src,
            dst_ref=dst,
            send_sem=ssem.at[n],
            recv_sem=rsem.at[n],
            device_id=device,
            device_id_type=MESH,
        )
        copy.start()
        sent.append(copy)
        return copy

    barrier = pltpu.get_barrier_semaphore()
    friends = [dict(dy=a, dz=b) for a, b in PEERS]
    friends += [dict(dc=1), dict(dx=1), dict(dx=2), dict(dx=3)]
    for f in friends:
        pl.semaphore_signal(barrier, inc=1, device_id=at(**f), device_id_type=MESH)
    pl.semaphore_wait(barrier, len(friends))

    t_near, t_far = [], []
    for d in (1, 2, 3):
        t_near.append(send(table, tt.at[dp], along(1, d)))
        t_near.append(send(table, tt.at[dp], along(0, d)))
    z_one = {d: send(pts.at[:, 0], zg[d], along(1, d)) for d in (1, 3)}
    y_one = {d: send(pts.at[:, 1], yg[d], along(0, d)) for d in (1, 3)}
    c_one = {d: send(cen, c_all.at[d], along(2, d)) for d in (1, 3)}
    tt[dp] = table[...]
    c_all[0] = cen[...]
    z_all[0, 0, 0] = zin[...]

    arrive = {}

    def slots(r):
        from_z = own if r == 0 else tts.at[y * 4 + (z - r) % 4]
        from_y = own if r == 0 else tts.at[((y - r) % 4) * 4 + z]
        for d in (2, 1, 3, 0):
            for k in range(2):
                group = ((y + d) % 4) * 4 + z
                pick = from_z[0, group * CAP + k]
                block = pts[pick, 0] if r == 0 else zg[r][pick]
                if d == 0:
                    x_all[r, k, c, 0] = block
                else:
                    outz[r, d - 1, k] = block
                group = y * 4 + (z + d) % 4
                pick = from_y[0, group * CAP + k]
                block = pts[pick, 1] if r == 0 else yg[r][pick]
                if d == 0:
                    x_all[r * 4, k, c, 1] = block
                else:
                    outy[r, d - 1, k] = block
            if d != 0:
                arrive[d, r, 0] = send(
                    outz.at[r, d - 1], x_all.at[d * 4 + r, :, c, 0], along(0, d)
                )
                arrive[r, d, 1] = send(
                    outy.at[r, d - 1], x_all.at[r * 4 + d, :, c, 1], along(1, d)
                )

    slots(0)
    for a, b in PEERS:
        if a and b:
            t_far.append(send(table, tt.at[dp], at(dy=a, dz=b)))
    zx = {d: send(zin, z_all.at[0, 0, d], along(2, d)) for d in (1, 2, 3)}
    for t in t_near + t_far:
        t.wait_recv()
    tt_copy = send(tt, tt_sib, at(dc=1))
    local = pltpu.make_async_copy(tt, tts, lsem.at[0])
    local.start()
    local.wait()
    z_one[1].wait_recv()
    z_fwd = [send(zg[1].at[0:4], zg[2].at[0:4], along(1, 1))]
    y_one[1].wait_recv()
    y_fwd = [send(yg[1].at[0:4], yg[2].at[0:4], along(0, 1))]
    z_one[3].wait_recv()
    z_fwd.append(send(zg[3].at[4:8], zg[2].at[4:8], along(1, 3)))
    y_one[3].wait_recv()
    y_fwd.append(send(yg[3].at[4:8], yg[2].at[4:8], along(0, 3)))
    c_one[1].wait_recv()
    c_fwd = [send(c_all.at[1, 0:128], c_all.at[2, 0:128], along(2, 1))]
    c_one[3].wait_recv()
    c_fwd.append(send(c_all.at[3, 128:256], c_all.at[2, 128:256], along(2, 3)))
    slots(1)
    slots(3)
    for copy in z_fwd + y_fwd:
        copy.wait_recv()
    slots(2)
    for copy in c_fwd:
        copy.wait_recv()

    centres = c_all[...].reshape(1024, 1024)
    sq[...] = (
        jnp.sum(jnp.square(centres.astype(F32)), 1, keepdims=True) * (1.0 / 64.0)
        + jnp.zeros((1024, 128), F32)
    )

    def score_chunk(i, carry):
        dy, dz = source_of(i)
        s = dy * 4 + dz
        s_abs = ((y - dy) % 4) * 4 + (z - dz) % 4
        rows = x_all[s].reshape(256, 1024)
        product = nt(c_all[...].reshape(1024, 1024), rows)
        for k in range(2):
            half = product[:, k * 128:(k + 1) * 128] * (1.0 / 32.0) - sq[...]
            peak = jnp.max(half, 0, keepdims=True)
            raised = jnp.exp(half - peak)
            scores[s * 2 + k] = raised.reshape(4, 4, 4, 16, 128)
            total = jnp.sum(raised, 0, keepdims=True)
            peaks[k, pl.ds(s_abs, 1), :] = peak
            st[k, pl.ds(s_abs, 1), :] = peak + jnp.log(total)
        return carry

    sib = {}

    def forward(group):
        for dy, dz in group:
            s = dy * 4 + dz
            if dy:
                arrive[dy, dz, 0].wait_recv()
            if dz:
                arrive[dy, dz, 1].wait_recv()
            sib[dy, dz] = send(x_all.at[s, :, c], x_all.at[s, :, c], at(dc=1))

    def score(lo, hi):
        for p in ORDER[lo:hi]:
            sib[p].wait_recv()
        lax.fori_loop(lo, hi, score_chunk, 0)

    forward(ORDER[0:5])
    forward(ORDER[5:9])
    score(0, 5)
    forward(ORDER[9:11])
    score(5, 9)
    forward(ORDER[11:15])
    score(9, 11)
    score(11, 14)
    forward(ORDER[15:])
    score(14, 15)
    score(15, 16)

    st_copy = send(st, sto, at(dc=1))
    st_copy.wait_recv()
    stc[...] = log_add(st[...], sto[...])
    g_copies = [send(stc, g_all.at[dp], at(dy=a, dz=b)) for a, b in PEERS]
    g_all[dp] = stc[...]
    for copy in zx.values():
        copy.wait_recv()
    for copy in g_copies:
        copy.wait_recv()
    zz = [send(z_all.at[0, 0], z_all.at[0, d], along(1, d)) for d in (1, 2, 3)]
    tt_copy.wait_recv()
    lane = lax.broadcasted_iota(jnp.int32, (16, 128), 1)
    mine = lane // 64 == c
    wide = lax.broadcasted_iota(jnp.int32, (16, 512), 1).astype(F32)
    source = lax.broadcasted_iota(jnp.int32, (16, 1), 0).astype(F32)
    table_rows = g_all[...].reshape(512, 128)

    def other_group(tables_of, k):
        partner = tables_of[:, 1, :].astype(F32)
        slot = jnp.sum(jnp.where(lane == dp * CAP + k, partner, 0.0), 1, keepdims=True)
        match = (wide == slot * 16.0 + source).astype(F32)
        other = jnp.dot(
            match, table_rows, precision=lax.Precision.HIGHEST, preferred_element_type=F32
        )
        return jnp.where(slot >= 0.0, log_add(stc[k], other), BIG)

    for k in range(2):
        total = jnp.where(mine, other_group(tt, k), other_group(tt_sib, k))
        alpha[k] = jnp.exp(peaks[k] - total)

    def weigh(r):
        def one(s, carry):
            dy, dz = s // 4, s % 4
            s_abs = ((y - dy) % 4) * 4 + (z - dz) % 4
            for k in range(2):
                col = pl.multiple_of(s * 256 + k * 128, 128)
                row = alpha[k, pl.ds(s_abs, 1), :]
                w_buf[:, pl.ds(col, 128)] = (
                    scores[s * 2 + k, r].reshape(256, 128) * row
                ).astype(BF16)
            return carry

        lax.fori_loop(0, 16, one, 0)
        mass[r] = nt(jnp.ones((8, 4096), BF16), w_buf[...])

        def tile(n, carry):
            col = pl.multiple_of(n * 256, 256)
            rows = x_all[:, :, :, :, :, pl.ds(col, 256)].reshape(4096, 256)
            sums[r, :, pl.ds(col, 256)] = nn(w_buf[...], rows)
            return carry

        lax.fori_loop(0, 4, tile, 0)

    lo, hi = slice(0, 128), slice(128, 256)

    def push(n, value, d):
        encode([value], [code_out.at[n]], scale_out.at[n])
        return (
            send(code_out.at[n], code_in.at[n], along(2, d)),
            send(scale_out.at[n], scale_in.at[n], along(2, d)),
        )

    def pull(n, copies):
        for copy in copies:
            copy.wait_recv()
        return decode([code_in.at[n]], scale_in.at[n])[0]

    weigh(2)
    via_a = push(0, sums[2, lo], 1)
    via_b = push(1, sums[2, hi], 3)
    mass_a = send(mass.at[2], mass_in.at[0], along(2, 1))
    for copy in zz:
        copy.wait_recv()
    zy = [send(z_all.at[0], z_all.at[d], along(0, d)) for d in (1, 2, 3)]
    weigh(3)
    up_hi = push(3, sums[3, hi], 1)
    weigh(1)
    down_lo = push(4, sums[1, lo], 3)
    mass_down = send(mass.at[1], mass_in.at[2], along(2, 3))
    up_lo = push(2, sums[3, lo] + pull(0, via_a), 1)
    mass_a.wait_recv()
    mass[3] += mass_in[0]
    mass_up = send(mass.at[3], mass_in.at[1], along(2, 1))
    down_hi = push(5, sums[1, hi] + pull(1, via_b), 3)
    weigh(0)
    for copy in zy:
        copy.wait_recv()
    zsq[...] = (
        jnp.sum(
            jnp.square(z_all[...].reshape(1024, 1024).astype(F32)), 1, keepdims=True
        ) * (1.0 / 16.0)
        + jnp.zeros((1024, 128), F32)
    )
    mass_down.wait_recv()
    mass_up.wait_recv()
    own_mass = jnp.transpose(mass[0] + mass_in[1] + mass_in[2])[:, 0:1]
    for rows, above, n_above, below, n_below in (
        (hi, up_hi, 3, down_hi, 5),
        (lo, up_lo, 2, down_lo, 4),
    ):
        total = sums[0, rows] + pull(n_above, above) + pull(n_below, below)
        above_line = total + PRIOR * cen[rows].astype(F32)
        below_line = own_mass[rows] + PRIOR
        one_out[rows] = above_line
        den_out[rows] = below_line + jnp.zeros((128, 128), F32)
        value = above_line / below_line
        ch[0, 0, rows] = value.astype(BF16)
        ch[0, 1, rows] = (value - ch[0, 0, rows].astype(F32)).astype(BF16)

    ch_copy = send(ch.at[0], ch.at[1], at(dc=1))

    def top_scores(h, carry):
        zs = z_all[...].reshape(1024, 1024)
        product = nt(zs, ch[h, 0]) + nt(zs, ch[h, 1])
        for k in range(2):
            cols = slice(k * 128, (k + 1) * 128)
            half = product[:, cols] * (1.0 / 8.0) - zsq[...]
            peak = jnp.max(half, 0, keepdims=True)
            raised = jnp.exp(half - peak)
            scores[16 + h * 2 + k] = raised.reshape(4, 4, 4, 16, 128)
            stat[h, 0:1, cols] = peak
            stat[h, 1:2, cols] = jnp.sum(raised, 0, keepdims=True)
        return carry

    lax.fori_loop(0, 1, top_scores, 0)
    ch_copy.wait_recv()
    lax.fori_loop(1, 2, top_scores, 0)
    stat_copy = send(stat, stat_in, at(dc=1))
    stat_copy.wait_recv()
    mass_two = jnp.zeros((1024, 1), F32)
    for h in range(2):
        peak = jnp.maximum(stat[h, 0:1], stat_in[1 - h, 0:1])
        mine_up = jnp.exp(stat[h, 0:1] - peak)
        total = stat[h, 1:2] * mine_up + stat_in[1 - h, 1:2] * jnp.exp(
            stat_in[1 - h, 0:1] - peak
        )
        scale = mine_up / total
        for k in range(2):
            part = slice(k * 128, (k + 1) * 128)
            weight = (
                scores[16 + h * 2 + k].reshape(1024, 128) * scale[:, part]
            )
            cols = slice(h * 256 + k * 128, h * 256 + (k + 1) * 128)
            wh[:, cols] = weight.astype(BF16)
            wl[:, cols] = (weight - wh[:, cols].astype(F32)).astype(BF16)
            mass_two = mass_two + jnp.sum(weight, 1, keepdims=True)
    def top_part(q):
        width = 384 if q < 2 else 256
        cols = slice(q * 384, q * 384 + width)
        hi_rows = ch[:, 0, :, cols].reshape(512, width)
        lo_rows = ch[:, 1, :, cols].reshape(512, width)
        part = nn(wh[...], hi_rows) + nn(wl[...], hi_rows) + nn(wh[...], lo_rows)
        for k in range(width // 128):
            scores[q * 3 + k] = part[:, k * 128:(k + 1) * 128].reshape(4, 4, 4, 16, 128)
        if q == 2:
            scores[8] = (mass_two + jnp.zeros((1024, 128), F32)).reshape(
                4, 4, 4, 16, 128
            )

    halves = (None, ha1, ha2)
    fulls = (None, fu1, fu2)

    def chunk(q, stage, r, half=None):
        where = [slice(None)] * 3
        for done in AXES_OF[q][:stage]:
            where[done] = 0
        where[AXES_OF[q][stage]] = r
        if half is not None:
            if stage < 2:
                free = min(AXES_OF[q][stage + 1:])
                where[free] = pl.ds(half * 2, 2)
            else:
                where.append(pl.ds(half * 8, 8))
        return scores.at[(pl.ds(q * 3, 3), *where)]

    def part_of(ref, stage, half):
        size = 2 if stage < 2 else 8
        return ref.at[:, pl.ds(half * size, size)]

    def top_push(q, n, r, half, d):
        axis = AXES_OF[q][0]
        value = chunk(q, 0, r, half)[...].reshape(3, 128, 128)
        encode(
            [value[b] for b in range(3)],
            [t_code.at[q, n, b] for b in range(3)],
            t_scale.at[q, n],
        )
        return (
            send(t_code.at[q, n], t_code_in.at[q, n], along(axis, d)),
            send(t_scale.at[q, n], t_scale_in.at[q, n], along(axis, d)),
        )

    def top_pull(q, n, copies, r, half):
        for copy in copies:
            copy.wait_recv()
        view = chunk(q, 0, r, half)
        parts = decode(
            [t_code_in.at[q, n, b] for b in range(3)], t_scale_in.at[q, n]
        )
        view[...] += jnp.stack(parts, 0).reshape(view.shape)

    via = []
    for q in (2, 0, 1):
        top_part(q)
        via.append((q, (top_push(q, 0, 2, 0, 1), top_push(q, 1, 2, 1, 3))))
    via = dict(via)
    early = [(top_push(q, 3, 3, 1, 1), top_push(q, 4, 1, 0, 3)) for q in range(3)]
    late = []
    for q in range(3):
        top_pull(q, 0, via[q][0], 3, 0)
        up = top_push(q, 2, 3, 0, 1)
        top_pull(q, 1, via[q][1], 1, 1)
        late.append((up, top_push(q, 5, 1, 1, 3)))
    for q in range(3):
        top_pull(q, 3, early[q][0], 0, 1)
        top_pull(q, 4, early[q][1], 0, 0)
        top_pull(q, 2, late[q][0], 0, 0)
        top_pull(q, 5, late[q][1], 0, 1)

    for stage in range(1, 3):
        ha, fu = halves[stage], fulls[stage]
        first, second = {}, {}
        for q in range(3):
            axis = AXES_OF[q][stage]
            first[q] = (
                send(chunk(q, stage, 2, 0), ha.at[q, 0], along(axis, 1)),
                send(chunk(q, stage, 2, 1), ha.at[q, 1], along(axis, 3)),
            )
        for q in range(3):
            axis = AXES_OF[q][stage]
            second[q] = [
                send(chunk(q, stage, 3, 1), part_of(fu.at[q, 0], stage, 1), along(axis, 1)),
                send(chunk(q, stage, 1, 0), part_of(fu.at[q, 1], stage, 0), along(axis, 3)),
            ]
        for q in range(3):
            axis = AXES_OF[q][stage]
            first[q][0].wait_recv()
            view = chunk(q, stage, 3, 0)
            view[...] += ha[q, 0]
            second[q].append(send(view, part_of(fu.at[q, 0], stage, 0), along(axis, 1)))
            first[q][1].wait_recv()
            view = chunk(q, stage, 1, 1)
            view[...] += ha[q, 1]
            second[q].append(send(view, part_of(fu.at[q, 1], stage, 1), along(axis, 3)))
        for q in range(3):
            for copy in second[q]:
                copy.wait_recv()
            view = chunk(q, stage, 0)
            view[...] += fu[q, 0] + fu[q, 1]
    denominator = scores[8, 0, 0, 0, :, 0:1] + PRIOR
    for q in range(8):
        cols = slice(q * 128, (q + 1) * 128)
        two_out[:, cols] = (
            scores[q, 0, 0, 0] + PRIOR * zin[:, cols].astype(F32)
        ) / denominator
    assert counter[0] <= ssem.shape[0]
    for copy in sent:
        copy.wait_send()


def tables(candidates):
    targets = candidates.reshape(-1)
    count = targets.shape[0]
    position = jnp.arange(count, dtype=jnp.int32)
    earlier = (targets[None, :] == targets[:, None]) & (
        position[None, :] < position[:, None]
    )
    slot = targets * CAP + jnp.sum(earlier.astype(jnp.int32), 1)
    mate = jnp.stack([slot[1::2], slot[0::2]], 1).reshape(-1)
    lanes = jnp.arange(128, dtype=jnp.int32)
    hit = slot[:, None] == lanes[None, :]
    block = jnp.sum(jnp.where(hit, (position // 2)[:, None], 0), 0)
    partner = jnp.sum(jnp.where(hit, mate[:, None] + 1, 0), 0) - 1
    rest = jnp.zeros((6, 128), jnp.int32)
    return jnp.concatenate([block[None], partner[None], rest], 0)


def local(points, candidates, level_one, level_two):
    vmem = pl.BlockSpec(memory_space=pltpu.VMEM)
    n_copies = 190
    dma = pltpu.SemaphoreType.DMA
    scratch = [
        pltpu.VMEM((16, 8, 128), jnp.int32),
        pltpu.VMEM((16, 8, 128), jnp.int32),
        pltpu.SMEM((16, 8, 128), jnp.int32),
        *[pltpu.VMEM((8, 32, 1024), BF16)] * 3,
        *[pltpu.VMEM((8, 32, 1024), BF16)] * 3,
        pltpu.VMEM((4, 3, 2, 32, 1024), BF16),
        pltpu.VMEM((4, 3, 2, 32, 1024), BF16),
        pltpu.VMEM((16, 2, 2, 2, 32, 1024), BF16),
        pltpu.VMEM((4, 256, 1024), BF16),
        pltpu.VMEM((1024, 128), F32),
        pltpu.VMEM((32, 4, 4, 4, 16, 128), F32),
        pltpu.VMEM((2, 16, 128), F32),
        pltpu.VMEM((2, 16, 128), F32),
        pltpu.VMEM((2, 16, 128), F32),
        pltpu.VMEM((16, 2, 16, 128), F32),
        pltpu.VMEM((2, 16, 128), F32),
        pltpu.VMEM((2, 16, 128), F32),
        pltpu.VMEM((256, 4096), BF16),
        pltpu.VMEM((4, 256, 1024), F32),
        *[pltpu.VMEM((6, 128, 1024), jnp.int16)] * 2,
        *[pltpu.VMEM((6, 8, 128), F32)] * 2,
        pltpu.VMEM((4, 8, 256), F32),
        pltpu.VMEM((3, 8, 256), F32),
        pltpu.VMEM((4, 4, 4, 16, 1024), BF16),
        pltpu.VMEM((1024, 128), F32),
        pltpu.VMEM((2, 2, 256, 1024), BF16),
        pltpu.VMEM((2, 8, 256), F32),
        pltpu.VMEM((2, 8, 256), F32),
        pltpu.VMEM((1024, 512), BF16),
        pltpu.VMEM((1024, 512), BF16),
        *[pltpu.VMEM((3, 6, 3, 128, 128), jnp.int16)] * 2,
        *[pltpu.VMEM((3, 6, 8, 128), F32)] * 2,
        pltpu.VMEM((3, 2, 3, 2, 16, 128), F32),
        pltpu.VMEM((3, 2, 3, 4, 16, 128), F32),
        pltpu.VMEM((3, 2, 3, 8, 128), F32),
        pltpu.VMEM((3, 2, 3, 16, 128), F32),
        dma((n_copies,)),
        dma((n_copies,)),
        dma((1,)),
    ]
    table = tables(candidates)
    one, den, two = pl.pallas_call(
        step_kernel,
        out_shape=(
            jax.ShapeDtypeStruct((256, 1024), F32),
            jax.ShapeDtypeStruct((256, 128), F32),
            jax.ShapeDtypeStruct((16, 1024), F32),
        ),
        in_specs=[vmem, vmem, vmem, pl.BlockSpec(memory_space=pltpu.SMEM), vmem],
        out_specs=(vmem, vmem, vmem),
        scratch_shapes=scratch,
        compiler_params=pltpu.CompilerParams(
            collective_id=0, has_side_effects=True, vmem_limit_bytes=62 * 2**20
        ),
        name="lloyd_step",
    )(points.reshape(8, 2, 32, 1024), level_one, table, table, level_two)
    return one / den[:, 0:1], two


def solution(mesh):
    placed = P(("dp", "cent"), None)
    return jax.shard_map(
        local,
        mesh=mesh,
        in_specs=(placed,) * 4,
        out_specs=(placed, placed),
        check_vma=False,
    )
```
